512 devices in a mesh: dp: 32 (over x, z_hi, core), mp: 16 (over z_lo, y).
Axes of the slice: x: 4, y: 8, z: 8 (z_hi: 4, z_lo: 2; z = z_hi * 2 + z_lo), core: 2. Of those that a mesh axis runs over, the one named last changes fastest.
Arguments:
- img_tokens: bfloat16 [512, 128, 1408], P(('dp', 'mp')), may hold values from -6 to 6
- w_key: bfloat16 [1408, 2048], P(None, 'mp'), may hold values from -0.15625 to 0.15625
- w_value: bfloat16 [1408, 2048], P(None, 'mp'), may hold values from -0.15625 to 0.15625
- queries: bfloat16 [512, 32, 2048], P('dp', None, 'mp'), may hold values from -6 to 6
- lengths: int32 [512], P('dp'), may hold values from 1 to 32
- d_out: bfloat16 [512, 32, 2048], P('dp', None, 'mp'), may hold values from -6 to 6
- img_pooled: bfloat16 [512, 1408], P(('dp', 'mp')), may hold values from -40 to 40
- w_proj: bfloat16 [1408, 2048], P(None, 'mp'), may hold values from -0.19921875 to 0.19921875
- txt_embed: bfloat16 [512, 2048], P('dp', 'mp'), may hold values from -80 to 80
- inv_temp: float32 [1], replicated, may hold values from 30 to 100
Outputs:
- attended: bfloat16 [512, 32, 2048], P('dp', None, 'mp')
- grad_queries: bfloat16 [512, 32, 2048], P('dp', None, 'mp')
- dw_key: float32 [1408, 2048], P('dp', 'mp')
- dw_value: float32 [1408, 2048], P('dp', 'mp')
- contrast: float32 [2, 512], P(None, 'dp')
The draws below stay inside these ranges and needn't reach their ends.
Inputs may be any that keep to these rules, and one draw needn't show every extreme that they name: lengths: each caption's count of real positions.
All inputs are finite; a program needn't handle non-finite values.
Results may differ from the reference program's by a relative error of at most 0.0081.
Values may be sent and summed in bfloat16 or wider, within the bound.
A program may use at most 64 MiB of HBM per device.

```python
import math
import jax
import jax.numpy as jnp
from jax import lax

D = 2048
DI = 1408
HEADS = 16
HD = 128
NTOK = 128
LQ = 32
GROUP = 16
BATCH = 512


def joint_embeddings(key):
    subkeys = [jax.random.fold_in(key, 7001 + n) for n in range(10)]
    centers = jax.random.normal(subkeys[0], (16, DI), jnp.float32)
    strengths = jnp.exp(jax.random.uniform(subkeys[1], (16,), jnp.float32, math.log(0.3), 0.0))
    drawn = jax.random.randint(subkeys[2], (BATCH,), 0, 64)
    member = drawn * drawn // 256
    one_hot = (member[:, None] == jnp.arange(16)[None, :]).astype(jnp.float32)
    picked = jnp.dot(one_hot, centers * strengths[:, None])
    mixing = jax.random.uniform(subkeys[3], (BATCH, 1), jnp.float32, 0.15, 0.6)
    w_proj = jnp.clip(jax.random.normal(subkeys[4], (DI, D), jnp.float32) * DI ** (-0.5), -0.19921875, 0.19921875)
    noise_part = jax.random.normal(subkeys[5], (BATCH, DI), jnp.float32)
    pooled = jnp.clip(picked + noise_part, -8.0, 8.0)
    projected = jnp.dot(pooled, w_proj)
    direction = projected * jax.lax.rsqrt(jnp.sum(projected * projected, axis=1, keepdims=True) + 1e-06)
    aligned = mixing * math.sqrt(D) * direction
    text_noise = jax.random.normal(subkeys[8], (BATCH, D), jnp.float32)
    text = jnp.clip(aligned + text_noise, -8.0, 8.0)
    return (pooled, w_proj, text)


def draw_img_pooled(key, part):
    return joint_embeddings(key)[0].astype(jnp.bfloat16)


def draw_w_proj(key, part):
    return joint_embeddings(key)[1].astype(jnp.bfloat16)


def draw_txt_embed(key, part):
    return joint_embeddings(key)[2].astype(jnp.bfloat16)


def place_ends(result, rng, low, high):
    longest = result.shape.index(max(result.shape))
    spots = []
    for shift in (0, 1):
        where = [jax.random.randint(jax.random.fold_in(rng, axis), (), 0, length) for axis, length in enumerate(result.shape)]
        where[longest] = (where[longest] + shift) % result.shape[longest]
        spots.append(tuple(where))
    return result.at[spots[0]].set(low).at[spots[1]].set(high)


def shard_levels(stream_key, dims, cuts, smallest, largest):
    def one(axis_at, shards_of):
        draws = jax.random.uniform(jax.random.fold_in(jax.random.fold_in(stream_key, 6), axis_at), (shards_of,), jnp.float32, smallest / len(cuts), largest / len(cuts))
        return jnp.repeat(jnp.exp(draws), dims[axis_at] // shards_of).reshape((-1,) + (1,) * (len(dims) - axis_at - 1))

    level = one(*cuts[0])
    for cut in cuts[1:]:
        level = level * one(*cut)
    return level


def gaussian(own_key, dims, deviation, reach, pieces=(), kind=jnp.bfloat16):
    gain = shard_levels(own_key, dims, pieces, -0.22, 0.18) if pieces else 1.0
    entries = jax.random.normal(own_key, dims, jnp.float32) * deviation * gain
    return jnp.minimum(jnp.maximum(entries, -reach), reach).astype(kind)


def setup_inputs(seed: int = 0) -> dict:
    seeds = jax.random.split(jax.random.key(seed), 11)
    return {
        "img_tokens": gaussian(seeds[0], (BATCH, NTOK, DI), 1.0, 6.0, ((0, 512),)),
        "w_key": gaussian(seeds[1], (DI, D), DI ** -0.5, 0.15625, ((1, 16),)),
        "w_value": gaussian(seeds[2], (DI, D), DI ** -0.5, 0.15625, ((1, 16),)),
        "queries": gaussian(seeds[3], (BATCH, LQ, D), 1.0, 6.0, ((0, 32), (2, 16))),
        "lengths": place_ends(jax.random.randint(seeds[4], (BATCH,), 1, LQ + 1), jax.random.fold_in(seeds[4], 1), 1, LQ).astype(jnp.int32),
        "d_out": gaussian(seeds[5], (BATCH, LQ, D), 1.0, 6.0, ((0, 32), (2, 16))),
        "img_pooled": draw_img_pooled(jax.random.fold_in(seeds[10], 71), 0),
        "w_proj": draw_w_proj(jax.random.fold_in(seeds[10], 71), 0),
        "txt_embed": draw_txt_embed(jax.random.fold_in(seeds[10], 71), 0),
        "inv_temp": jnp.clip(jnp.exp(jax.random.uniform(seeds[9], (1,), jnp.float32, math.log(30.0), math.log(100.0))), 30.0, 100.0),
    }


def attend_block(tokens, queries, lengths, d_out, w_key, w_value):
    count = tokens.shape[0]
    flat = tokens.reshape(count * NTOK, DI)
    keys = jnp.dot(flat, w_key, preferred_element_type=jnp.float32).astype(jnp.bfloat16).reshape(count, NTOK, HEADS, HD)
    values = jnp.dot(flat, w_value, preferred_element_type=jnp.float32).astype(jnp.bfloat16).reshape(count, NTOK, HEADS, HD)
    query_heads = queries.reshape(count, LQ, HEADS, HD).astype(jnp.float32)
    inv_root = HD ** (-0.5)
    scores = jnp.einsum('blhd,bthd->bhlt', query_heads, keys.astype(jnp.float32)) * inv_root
    probs = jax.nn.softmax(scores, axis=-1)
    probs_b = probs.astype(jnp.bfloat16).astype(jnp.float32)
    keep_rows = (jnp.arange(LQ)[None, :] < lengths[:, None]).astype(jnp.float32)
    output = jnp.einsum('bhlt,bthd->blhd', probs_b, values.astype(jnp.float32)) * keep_rows[:, :, None, None]
    attended = output.reshape(count, LQ, D).astype(jnp.bfloat16)
    masked = (d_out.astype(jnp.float32) * keep_rows[:, :, None]).astype(jnp.bfloat16)
    grad_heads = masked.reshape(count, LQ, HEADS, HD).astype(jnp.float32)
    grad_values = jnp.einsum('bhlt,blhd->bthd', probs_b, grad_heads).astype(jnp.bfloat16)
    grad_probs = jnp.einsum('blhd,bthd->bhlt', grad_heads, values.astype(jnp.float32))
    row_dots = lax.optimization_barrier(jnp.sum(probs * grad_probs, axis=-1, keepdims=True))
    grad_scores = (probs * (grad_probs - row_dots) * inv_root).astype(jnp.bfloat16).astype(jnp.float32)
    grad_queries = jnp.einsum('bhlt,bthd->blhd', grad_scores, keys.astype(jnp.float32)).reshape(count, LQ, D).astype(jnp.bfloat16)
    grad_keys = jnp.einsum('bhlt,blhd->bthd', grad_scores, query_heads).astype(jnp.bfloat16)
    key_terms = jnp.dot(flat.T, grad_keys.reshape(count * NTOK, D), preferred_element_type=jnp.float32)
    value_terms = jnp.dot(flat.T, grad_values.reshape(count * NTOK, D), preferred_element_type=jnp.float32)
    return (attended, grad_queries, key_terms, value_terms)

def reference(img_tokens, w_key, w_value, queries, lengths, d_out, img_pooled, w_proj, txt_embed, inv_temp):
    blocks = BATCH // GROUP
    tok_blocks = img_tokens.reshape(blocks, GROUP, NTOK, DI)
    query_blocks = queries.reshape(blocks, GROUP, LQ, D)
    length_blocks = lengths.reshape(blocks, GROUP)
    grad_blocks = d_out.reshape(blocks, GROUP, LQ, D)

    def step(carry, inputs):
        attended, grad_queries, key_terms, value_terms = attend_block(inputs[0], inputs[1], inputs[2], inputs[3], w_key, w_value)
        return ((carry[0] + key_terms, carry[1] + value_terms), (attended, grad_queries))
    start = (jnp.zeros((DI, D), jnp.float32), jnp.zeros((DI, D), jnp.float32))
    sums, outputs = lax.scan(step, start, (tok_blocks, query_blocks, length_blocks, grad_blocks))
    attended = outputs[0].reshape(BATCH, LQ, D)
    grad_queries = outputs[1].reshape(BATCH, LQ, D)
    img_raw = jnp.dot(img_pooled, w_proj, preferred_element_type=jnp.float32).astype(jnp.bfloat16)
    img_sq = lax.optimization_barrier(jnp.sum(jnp.square(img_raw.astype(jnp.float32)), axis=1))
    txt_sq = lax.optimization_barrier(jnp.sum(jnp.square(txt_embed.astype(jnp.float32)), axis=1))
    dots = jnp.dot(img_raw, txt_embed.T, preferred_element_type=jnp.float32)
    logits = inv_temp[0] * dots * lax.rsqrt(img_sq + 1e-06)[:, None] * lax.rsqrt(txt_sq + 1e-06)[None, :]
    diagonal = jnp.diagonal(logits)
    image_side = jax.nn.logsumexp(logits, axis=1) - diagonal
    caption_side = jax.nn.logsumexp(logits, axis=0) - diagonal
    contrast = jnp.stack([image_side, caption_side])
    return (attended, grad_queries, sums[0], sums[1], contrast)
```

```python
import functools

import jax
import jax.numpy as jnp
from jax import lax
from jax.experimental import pallas as pl
from jax.experimental.pallas import tpu as pltpu
from jax.sharding import PartitionSpec as P

HD = 128
NX, NZH, NC, NZL, NY = 4, 4, 2, 2, 8
DI = 1408
ROOT = HD ** (-0.5)
MESH = pl.DeviceIdType.MESH
F32 = jnp.float32
BF16 = jnp.bfloat16


def nt(a, b):
    return lax.dot_general(a, b, (((1,), (1,)), ((), ())), preferred_element_type=F32)


def tn(a, b):
    return lax.dot_general(a, b, (((0,), (0,)), ((), ())), preferred_element_type=F32)


def nn(a, b):
    return jnp.dot(a, b, preferred_element_type=F32)


def kernel(
    tok, wk, wv, q, length, do, pooled, wp, txt, temp,
    att, gq, dwk, dwv, con,
    ring, w, qp, dop, att_s, gq_s, att_r, gq_r, acc,
    s1, r1, own2, s2, r2, s3, r3, t3, s4, r4, s5, r5,
    prow, gbuf, pk, rk, zs, zr, cs, cr,
    ring_ss, ring_rs, z_ss, z_rs, w_ss, w_rs, c1_ss, c1_rs, c2_ss, c2_rs, c3_ss, c3_rs,
    c4_ss, c4_rs, c5_ss, c5_rs, c6_ss, c6_rs, t1_ss, t1_rs, t2_ss, t2_rs, t3_ss, t3_rs,
    t4_ss, t4_rs, t5_ss, t5_rs,
):
    d = lax.axis_index("dp")
    m = lax.axis_index("mp")
    x, zh, c = d // (NZH * NC), lax.rem(d // NC, NZH), lax.rem(d, NC)
    zl, y = m // NY, lax.rem(m, NY)

    def y_at(k):
        return lax.rem(y + k + NY, NY)

    def y_peer(k):
        return (d, zl * NY + y_at(k))

    def x_at(k):
        return lax.rem(x + k, NX)

    def x_peer(k):
        return (x_at(k) * (NZH * NC) + zh * NC + c, m)

    def h_at(k):
        return lax.rem(zh + k, NZH)

    def h_peer(k):
        return (x * (NZH * NC) + h_at(k) * NC + c, m)

    z_peer = (d, (1 - zl) * NY + y)
    c_peer = (d + 1 - 2 * c, m)

    def remote(src, dst, ss, rs, to):
        return pltpu.make_async_remote_copy(
            src_ref=src, dst_ref=dst, send_sem=ss, recv_sem=rs, device_id=to, device_id_type=MESH
        )

    sent = []

    def send(copy):
        copy.start()
        sent.append(copy)
        return copy

    barrier = pltpu.get_barrier_semaphore()
    peers = [y_peer(k) for k in range(1, NY)] + [z_peer, c_peer]
    peers += [x_peer(k) for k in range(1, NX)] + [h_peer(k) for k in range(1, NZH)]
    for peer in peers:
        pl.semaphore_signal(barrier, inc=1, device_id=peer, device_id_type=MESH)

    w[0, :, 0:HD] = wk[...]
    w[1, :, 0:HD] = wv[...]
    row = jnp.zeros((16, 128), F32)
    rows = lax.broadcasted_iota(jnp.int32, (16, 128), 0)
    for i in range(DI // 128):
        piece = pooled[0:1, i * 128 : (i + 1) * 128].astype(F32)
        row = jnp.where(rows == i, piece, row)
    prow[zl, y] = row
    s4[...] = jnp.zeros_like(s4)
    s5[...] = jnp.zeros_like(s5)

    pl.semaphore_wait(barrier, len(peers))

    def hop(way, dist, half):
        side = 0 if way > 0 else 1
        part = pl.ds(half * 64, 64)
        src = tok.at[part] if dist == 1 else ring.at[2 * (dist - 2) + side, part]
        slot = 6 if dist == 4 else 2 * (dist - 1) + side
        return remote(
            src, ring.at[slot, part], ring_ss.at[side, dist - 1, half], ring_rs.at[side, dist - 1, half],
            y_peer(way),
        )

    def arrive(dist, half):
        for way in (1, -1):
            if dist < 4 or (half == 0) == (way > 0):
                hop(way, dist, half).wait_recv()
                if dist < 3 or (dist == 3 and (half == 0) == (way > 0)):
                    send(hop(way, dist + 1, half))

    for half in (0, 1):
        for way in (1, -1):
            send(hop(way, 1, half))

    away = pl.ds((1 - zl) * NY, NY)
    here = pl.ds(zl * NY, NY)
    swap_q = send(remote(q.at[away], qp, z_ss.at[0], z_rs.at[0], z_peer))
    swap_do = send(remote(do.at[away], dop, z_ss.at[1], z_rs.at[1], z_peer))
    swap_w = send(remote(w.at[c, :, pl.ds(0, HD)], w.at[c, :, pl.ds(HD, HD)], w_ss.at[0], w_rs.at[0], z_peer))
    c1 = [send(remote(prow.at[zl, y], prow.at[zl, y], c1_ss.at[k], c1_rs.at[k], y_peer(k))) for k in range(1, NY)]

    def attend(count, sources, load, first):
        tokens = load()
        keys2 = nn(tokens, w[0]).astype(BF16)
        values2 = nn(tokens, w[1]).astype(BF16)
        spots = lax.broadcasted_iota(jnp.int32, (32, 128), 0)
        grads_k, grads_v = [], []
        for i in range(count):
            src = sources[i]
            b = zl * NY + src
            keep = spots < length[b]
            both_k, both_v = [], []
            for h in range(2):
                query = q[b] if h == 0 else qp[src]
                cot = do[b] if h == 0 else dop[src]
                part = slice(i * 128, (i + 1) * 128)
                cols = slice(h * HD, (h + 1) * HD)
                key, value = keys2[part, cols], values2[part, cols]
                scores = nt(query, key) * ROOT
                top = jnp.max(scores, axis=1, keepdims=True)
                e = jnp.exp(scores - top)
                probs = e / jnp.sum(e, axis=1, keepdims=True)
                probs_b = probs.astype(BF16)
                out = jnp.where(keep, nn(probs_b, value), 0.0).astype(BF16)
                masked = jnp.where(keep, cot.astype(F32), 0.0).astype(BF16)
                both_v.append(tn(probs_b, masked).astype(BF16))
                grad_probs = nt(masked, value)
                dots = jnp.sum(probs * grad_probs, axis=1, keepdims=True)
                grad_scores = (probs * (grad_probs - dots) * ROOT).astype(BF16)
                grad_q = nn(grad_scores, key).astype(BF16)
                both_k.append(tn(grad_scores, query).astype(BF16))
                if h == 0:
                    att[b] = out
                    gq[b] = grad_q
                else:
                    att_s[src] = out
                    gq_s[src] = grad_q
            grads_k.append(jnp.concatenate(both_k, axis=1))
            grads_v.append(jnp.concatenate(both_v, axis=1))
        grad_k = grads_k[0] if count == 1 else jnp.concatenate(grads_k, axis=0)
        grad_v = grads_v[0] if count == 1 else jnp.concatenate(grads_v, axis=0)
        for n, grad in ((0, grad_k), (1, grad_v)):
            term = tn(tokens, grad)
            if first:
                acc[n] = term
            else:
                acc[n] += term

    def pair(dist):
        lo = 2 * (dist - 1)
        attend(2, [y_at(-dist), y_at(dist)], lambda: ring[lo : lo + 2].reshape(256, DI), False)

    arrive(1, 0)
    for copy in c1:
        copy.wait_recv()
    c2 = send(remote(prow.at[zl], prow.at[zl], c2_ss, c2_rs, z_peer))

    arrive(1, 1)
    swap_w.wait_recv()
    share_w = send(remote(w.at[c, :, pl.ds(HD, HD)], w.at[c, :, pl.ds(HD, HD)], w_ss.at[1], w_rs.at[1], c_peer))
    remote(prow.at[zl], prow.at[1 - zl], c2_ss, c2_rs, z_peer).wait_recv()
    part = jnp.zeros((16, HD), F32)
    for i in range(DI // 128):
        piece = prow[:, :, i, :].reshape(16, 128).astype(BF16)
        part += nn(piece, wp[i * 128 : (i + 1) * 128, :])
    mine = jnp.concatenate([part.astype(BF16), txt[...]], axis=0)
    gbuf[x, zh, c] = mine
    c3a = send(remote(gbuf.at[x, zh, c], gbuf.at[x, zh, c], c3_ss.at[0], c3_rs.at[0], c_peer))
    swap_q.wait_recv()
    swap_do.wait_recv()
    c3a.wait_recv()
    c3b = [
        send(remote(gbuf.at[x, zh], gbuf.at[x, zh], c3_ss.at[k], c3_rs.at[k], x_peer(k))) for k in range(1, NX)
    ]
    share_w.wait_recv()

    attend(1, [y], lambda: tok[...], True)
    arrive(2, 0)
    for copy in c3b:
        copy.wait_recv()
    c3c = [
        send(remote(gbuf.at[:, zh], gbuf.at[:, zh], c3_ss.at[3 + k], c3_rs.at[3 + k], h_peer(k)))
        for k in range(1, NZH)
    ]
    arrive(2, 1)
    pair(1)
    arrive(3, 0)
    for copy in c3c:
        copy.wait_recv()
    every = gbuf[...].reshape(512 // 16, 32, HD)
    all_img = every[:, :16].reshape(512, HD)
    all_txt = every[:, 16:].reshape(512, HD)
    own = gbuf[x, zh, c]
    dots_img = nt(own[:16], all_txt)
    dots_txt = nt(own[16:], all_img)
    ones = jnp.ones((8, HD), F32)

    def squares(rows_):
        wide = rows_.astype(F32)
        return lax.dot_general(
            ones, wide * wide, (((1,), (1,)), ((), ())),
            preferred_element_type=F32, precision=lax.Precision.HIGHEST,
        )

    sq_img, sq_txt = squares(all_img), squares(all_txt)
    for k in range(NY):
        pk[k, 0:2] = dots_img[2 * k : 2 * k + 2]
        pk[k, 2:4] = dots_txt[2 * k : 2 * k + 2]
        pk[k, 4:6] = sq_img[4:6]
        pk[k, 6:8] = sq_txt[6:8]
    c4 = [
        send(remote(pk.at[y_at(k)], rk.at[k], c4_ss.at[k], c4_rs.at[k], y_peer(k))) for k in range(1, NY)
    ]
    pair(2)
    arrive(3, 1)
    total = pk[y]
    for k in range(1, NY):
        c4[k - 1].wait_recv()
        total += rk[k]
    zs[...] = total
    c5 = send(remote(zs, zr, c5_ss, c5_rs, z_peer))
    pair(3)
    c5.wait_recv()
    total = zs[...] + zr[...]
    spot = lax.broadcasted_iota(jnp.int32, (2, 512), 1)
    index = d * 16 + 2 * y + lax.broadcasted_iota(jnp.int32, (2, 512), 0)
    hit = spot == index
    sq_i, sq_t = total[4:5], total[6:7]

    def side(dots, sq_rows, sq_cols):
        sq_row = jnp.sum(jnp.where(hit, sq_rows, 0.0), axis=1, keepdims=True)
        logits = temp[0] * dots * lax.rsqrt(sq_row + 1e-6) * lax.rsqrt(sq_cols + 1e-6)
        top = jnp.max(logits, axis=1, keepdims=True)
        lse = top + jnp.log(jnp.sum(jnp.exp(logits - top), axis=1, keepdims=True))
        return lse - jnp.sum(jnp.where(hit, logits, 0.0), axis=1, keepdims=True)

    img_side = side(total[0:2], sq_i, sq_t)
    txt_side = side(total[2:4], sq_t, sq_i)
    lane = lax.broadcasted_iota(jnp.int32, (8, 128), 1)
    line = lax.broadcasted_iota(jnp.int32, (8, 128), 0)
    tile = jnp.zeros((8, 128), F32)
    for r in range(2):
        here_lane = lane == 2 * y + r
        tile = jnp.where(here_lane & (line == 0), img_side[r : r + 1], tile)
        tile = jnp.where(here_lane & (line == 1), txt_side[r : r + 1], tile)
    cs[...] = tile
    c6 = [send(remote(cs, cr.at[k], c6_ss.at[k], c6_rs.at[k], y_peer(k))) for k in range(1, NY)]

    arrive(4, 0)
    arrive(4, 1)
    attend(1, [y_at(4)], lambda: ring[6], False)

    back = [
        send(remote(att_s, att_r, z_ss.at[2], z_rs.at[2], z_peer)),
        send(remote(gq_s, gq_r, z_ss.at[3], z_rs.at[3], z_peer)),
    ]

    XR, HR, CR = DI // NX, DI // (NX * NZH), DI // (NX * NZH * NC)

    def block(k):
        return pl.ds(pl.multiple_of(x_at(k) * XR, 32), XR)

    order = (1, 2, 3, 0)
    t1 = {}
    for k in order:
        s1[block(k), :] = acc[1 - c, block(k), :].astype(BF16)
        t1[k] = send(remote(s1.at[block(k)], r1.at[block(k)], t1_ss.at[k], t1_rs.at[k], c_peer))
    t2 = {}
    for k in order:
        t1[k].wait_recv()
        both = acc[c, block(k), :] + r1[block(k), :].astype(F32)
        own2[k] = both[:, :HD]
        s2[k] = both[:, HD:].astype(BF16)
        t2[k] = send(remote(s2.at[k], r2.at[k], t2_ss.at[k], t2_rs.at[k], z_peer))
    t3c = {}
    for k in order[:3]:
        t2[k].wait_recv()
        s3[k] = (own2[k] + r2[k].astype(F32)).astype(BF16)
        t3c[k] = send(remote(s3.at[k], r3.at[k], t3_ss.at[k], t3_rs.at[k], x_peer(k)))
    t2[0].wait_recv()
    block_sum = own2[0] + r2[0].astype(F32)
    for k in order[:3]:
        t3c[k].wait_recv()
        block_sum += r3[k].astype(F32)
    t3[...] = block_sum
    t4 = []
    for k in range(1, NZH):
        s4[k, 0:HR] = t3[pl.ds(pl.multiple_of(h_at(k) * HR, 8), HR), :].astype(BF16)
        t4.append(send(remote(s4.at[k], r4.at[k], t4_ss.at[k], t4_rs.at[k], h_peer(k))))
    piece = t3[pl.ds(pl.multiple_of(zh * HR, 8), HR), :]
    for k in range(1, NZH):
        t4[k - 1].wait_recv()
        piece += r4[k, 0:HR].astype(F32)
    low, high = piece[:CR], piece[CR:]
    s5[0:CR] = jnp.where(c == 0, high, low)
    t5 = send(remote(s5, r5, t5_ss, t5_rs, c_peer))
    kept = jnp.where(c == 0, low, high)

    for copy in back:
        copy.wait_recv()
    att[away] = att_r[...]
    gq[away] = gq_r[...]
    answer = cs[...]
    for k in range(1, NY):
        c6[k - 1].wait_recv()
        answer += cr[k]
    con[...] = answer[0:2, 0:16]
    t5.wait_recv()
    got = r5[0:CR]
    dwk[...] = jnp.where(c == 0, kept, got)
    dwv[...] = jnp.where(c == 0, got, kept)
    for copy in sent:
        copy.wait_send()


def body(img_tokens, w_key, w_value, queries, lengths, d_out, img_pooled, w_proj, txt_embed, inv_temp):
    vmem = pl.BlockSpec(memory_space=pltpu.VMEM)
    smem = pl.BlockSpec(memory_space=pltpu.SMEM)
    dma = pltpu.SemaphoreType.DMA
    V = pltpu.VMEM
    return pl.pallas_call(
        kernel,
        out_shape=(
            jax.ShapeDtypeStruct((16, 32, HD), BF16),
            jax.ShapeDtypeStruct((16, 32, HD), BF16),
            jax.ShapeDtypeStruct((44, HD), F32),
            jax.ShapeDtypeStruct((44, HD), F32),
            jax.ShapeDtypeStruct((2, 16), F32),
        ),
        in_specs=[vmem, vmem, vmem, vmem, smem, vmem, vmem, vmem, vmem, smem],
        out_specs=(vmem,) * 5,
        scratch_shapes=[
            V((7, 128, DI), BF16),
            V((2, DI, 256), BF16),
            V((8, 32, HD), BF16),
            V((8, 32, HD), BF16),
            V((8, 32, HD), BF16),
            V((8, 32, HD), BF16),
            V((8, 32, HD), BF16),
            V((8, 32, HD), BF16),
            V((2, DI, 256), F32),
            V((DI, 256), BF16),
            V((DI, 256), BF16),
            V((4, 352, HD), F32),
            V((4, 352, HD), BF16),
            V((4, 352, HD), BF16),
            V((4, 352, HD), BF16),
            V((4, 352, HD), BF16),
            V((352, HD), F32),
            V((4, 96, HD), BF16),
            V((4, 96, HD), BF16),
            V((48, HD), F32),
            V((48, HD), F32),
            V((2, 8, 16, 128), F32),
            V((4, 4, 2, 32, HD), BF16),
            V((8, 8, 512), F32),
            V((8, 8, 512), F32),
            V((8, 512), F32),
            V((8, 512), F32),
            V((8, 128), F32),
            V((8, 8, 128), F32),
            dma((2, 4, 2)), dma((2, 4, 2)),
            dma((4,)), dma((4,)),
            dma((2,)), dma((2,)),
            dma((8,)), dma((8,)),
            dma, dma,
            dma((8,)), dma((8,)),
            dma((8,)), dma((8,)),
            dma, dma,
            dma((8,)), dma((8,)),
            dma((4,)), dma((4,)),
            dma((4,)), dma((4,)),
            dma((4,)), dma((4,)),
            dma((4,)), dma((4,)),
            dma, dma,
        ],
        compiler_params=pltpu.CompilerParams(
            collective_id=0, has_side_effects=True, vmem_limit_bytes=48 * 1024 * 1024
        ),
        cost_estimate=pl.CostEstimate(flops=6_200_000_000, bytes_accessed=4_000_000, transcendentals=100_000),
    )(
        img_tokens.reshape(128, DI), w_key, w_value, queries, lengths, d_out, img_pooled, w_proj, txt_embed, inv_temp
    )


def solution(mesh):
    placed = (
        P(("dp", "mp"), None, None),
        P(None, "mp"),
        P(None, "mp"),
        P("dp", None, "mp"),
        P("dp"),
        P("dp", None, "mp"),
        P(("dp", "mp"), None),
        P(None, "mp"),
        P("dp", "mp"),
        P(),
    )
    return jax.shard_map(
        body,
        mesh=mesh,
        in_specs=placed,
        out_specs=(
            P("dp", None, "mp"),
            P("dp", None, "mp"),
            P("dp", "mp"),
            P("dp", "mp"),
            P(None, "dp"),
        ),
        check_vma=False,
    )
```

```python
import functools

import jax
import jax.numpy as jnp
from jax import lax
from jax.experimental import pallas as pl
from jax.experimental.pallas import tpu as pltpu
from jax.sharding import PartitionSpec as P

HD = 128
NX, NZH, NC, NZL, NY = 4, 4, 2, 2, 8
DI = 1408
ROOT = HD ** (-0.5)
MESH = pl.DeviceIdType.MESH
F32 = jnp.float32
BF16 = jnp.bfloat16


def nt(a, b):
    return lax.dot_general(a, b, (((1,), (1,)), ((), ())), preferred_element_type=F32)


def tn(a, b):
    return lax.dot_general(a, b, (((0,), (0,)), ((), ())), preferred_element_type=F32)


def nn(a, b):
    return jnp.dot(a, b, preferred_element_type=F32)


def kernel(
    tok_in, wk, wv, q_in, length_in, do_in, pooled_in, wp_in, txt_in, temp,
    att, gq, dwk, dwv, con,
    tok, q, length, do, pooled, wp, txt, in_sem,
    ring, w, qp, dop, att_s, gq_s, att_r, gq_r, acc,
    s1, r1, own2, s2, r2, s3, r3, own_w, s3w, r3w, t3, s4, r4, s5, r5,
    prow, gbuf, pk, pz, pk2, rk, cs, cr,
    ring_ss, ring_rs, z_ss, z_rs, w_ss, w_rs, c1_ss, c1_rs, c2_ss, c2_rs, c3_ss, c3_rs,
    c4_ss, c4_rs, c5_ss, c5_rs, c6_ss, c6_rs, t1_ss, t1_rs, t2_ss, t2_rs, t3_ss, t3_rs,
    t4_ss, t4_rs, t5_ss, t5_rs,
):
    d = lax.axis_index("dp")
    m = lax.axis_index("mp")
    x, zh, c = d // (NZH * NC), lax.rem(d // NC, NZH), lax.rem(d, NC)
    zl, y = m // NY, lax.rem(m, NY)

    def y_at(k):
        return lax.rem(y + k + NY, NY)

    def y_peer(k):
        return (d, zl * NY + y_at(k))

    def x_at(k):
        return lax.rem(x + k, NX)

    def x_peer(k):
        return (x_at(k) * (NZH * NC) + zh * NC + c, m)

    def h_at(k):
        return lax.rem(zh + k, NZH)

    def h_peer(k):
        return (x * (NZH * NC) + h_at(k) * NC + c, m)

    z_peer = (d, (1 - zl) * NY + y)
    c_peer = (d + 1 - 2 * c, m)

    def remote(src, dst, ss, rs, to):
        return pltpu.make_async_remote_copy(
            src_ref=src, dst_ref=dst, send_sem=ss, recv_sem=rs, device_id=to, device_id_type=MESH
        )

    sent = []

    def send(copy):
        copy.start()
        sent.append(copy)
        return copy

    loads = [
        pltpu.make_async_copy(src, dst, in_sem.at[i])
        for i, (src, dst) in enumerate(
            (
                (wk, w.at[0, :, pl.ds(0, HD)]), (wv, w.at[1, :, pl.ds(0, HD)]), (pooled_in, pooled),
                (tok_in, tok), (q_in, q), (do_in, do), (wp_in, wp), (txt_in, txt), (length_in, length),
            )
        )
    ]
    for copy in loads:
        copy.start()

    barrier = pltpu.get_barrier_semaphore()
    peers = [y_peer(k) for k in range(1, NY)] + [z_peer, c_peer]
    peers += [x_peer(k) for k in range(1, NX)] + [h_peer(k) for k in range(1, NZH)]
    for peer in peers:
        pl.semaphore_signal(barrier, inc=1, device_id=peer, device_id_type=MESH)

    for copy in loads:
        copy.wait()
    row = jnp.zeros((16, 128), F32)
    rows = lax.broadcasted_iota(jnp.int32, (16, 128), 0)
    for i in range(DI // 128):
        piece = pooled[0:1, i * 128 : (i + 1) * 128].astype(F32)
        row = jnp.where(rows == i, piece, row)
    prow[zl, y] = row
    s4[...] = jnp.zeros_like(s4)
    s5[...] = jnp.zeros_like(s5)

    pl.semaphore_wait(barrier, len(peers))

    def hop(way, dist, half):
        side = 0 if way > 0 else 1
        part = pl.ds(half * 64, 64)
        src = tok_in.at[part] if dist == 1 else ring.at[2 * (dist - 2) + side, part]
        slot = 6 if dist == 4 else 2 * (dist - 1) + side
        return remote(
            src, ring.at[slot, part], ring_ss.at[side, dist - 1, half], ring_rs.at[side, dist - 1, half],
            y_peer(way),
        )

    def arrive(dist, half):
        for way in (1, -1):
            if dist < 4 or (half == 0) == (way > 0):
                hop(way, dist, half).wait_recv()
                if dist < 3 or (dist == 3 and (half == 0) == (way > 0)):
                    send(hop(way, dist + 1, half))

    c1 = [send(remote(prow.at[zl, y], prow.at[zl, y], c1_ss.at[k], c1_rs.at[k], y_peer(k))) for k in range(1, NY)]
    for half in (0, 1):
        for way in (1, -1):
            send(hop(way, 1, half))
    away = pl.ds((1 - zl) * NY, NY)
    swap_w = send(remote(w.at[c, :, pl.ds(0, HD)], w.at[c, :, pl.ds(HD, HD)], w_ss.at[0], w_rs.at[0], z_peer))
    swap_q = send(remote(q_in.at[away], qp, z_ss.at[0], z_rs.at[0], z_peer))
    swap_do = send(remote(do_in.at[away], dop, z_ss.at[1], z_rs.at[1], z_peer))

    def attend(count, sources, tokens):
        keys2 = nn(tokens, w[0]).astype(BF16)
        values2 = nn(tokens, w[1]).astype(BF16)
        spots = lax.broadcasted_iota(jnp.int32, (32, 128), 0)
        grads_k, grads_v = [], []
        for i in range(count):
            src = sources[i]
            b = zl * NY + src
            keep = spots < length[b]
            both_k, both_v = [], []
            for h in range(2):
                query = q[b] if h == 0 else qp[src]
                cot = do[b] if h == 0 else dop[src]
                part = slice(i * 128, (i + 1) * 128)
                cols = slice(h * HD, (h + 1) * HD)
                key, value = keys2[part, cols], values2[part, cols]
                scores = nt(query, key) * ROOT
                top = jnp.max(scores, axis=1, keepdims=True)
                e = jnp.exp(scores - top)
                probs = e / jnp.sum(e, axis=1, keepdims=True)
                probs_b = probs.astype(BF16)
                out = jnp.where(keep, nn(probs_b, value), 0.0).astype(BF16)
                masked = jnp.where(keep, cot.astype(F32), 0.0).astype(BF16)
                both_v.append(tn(probs_b, masked).astype(BF16))
                grad_probs = nt(masked, value)
                dots = jnp.sum(probs * grad_probs, axis=1, keepdims=True)
                grad_scores = (probs * (grad_probs - dots) * ROOT).astype(BF16)
                grad_q = nn(grad_scores, key).astype(BF16)
                both_k.append(tn(grad_scores, query).astype(BF16))
                if h == 0:
                    att[b] = out
                    gq[b] = grad_q
                else:
                    att_s[src] = out
                    gq_s[src] = grad_q
            grads_k.append(jnp.concatenate(both_k, axis=1))
            grads_v.append(jnp.concatenate(both_v, axis=1))
        grad_k = grads_k[0] if count == 1 else jnp.concatenate(grads_k, axis=0)
        grad_v = grads_v[0] if count == 1 else jnp.concatenate(grads_v, axis=0)
        return grad_k, grad_v

    def pair(dist):
        lo = 2 * (dist - 1)
        tokens = ring[lo : lo + 2].reshape(256, DI)
        grad_k, grad_v = attend(2, [y_at(-dist), y_at(dist)], tokens)
        acc[0] += tn(tokens, grad_k)
        acc[1] += tn(tokens, grad_v)

    arrive(1, 0)
    arrive(1, 1)
    for copy in c1:
        copy.wait_recv()
    c2 = send(remote(prow.at[zl], prow.at[zl], c2_ss, c2_rs, z_peer))
    swap_w.wait_recv()
    share_w = send(remote(w.at[c, :, pl.ds(HD, HD)], w.at[c, :, pl.ds(HD, HD)], w_ss.at[1], w_rs.at[1], c_peer))

    arrive(2, 0)
    swap_q.wait_recv()
    swap_do.wait_recv()
    share_w.wait_recv()
    grad_k, grad_v = attend(1, [y], tok[...])
    acc[0] = tn(tok[...], grad_k)
    acc[1] = tn(tok[...], grad_v)
    c2.wait_recv()
    part = jnp.zeros((16, HD), F32)
    for i in range(DI // 128):
        piece = prow[:, :, i, :].reshape(16, 128).astype(BF16)
        part += nn(piece, wp[i * 128 : (i + 1) * 128, :])
    gbuf[x, zh, c] = jnp.concatenate([part.astype(BF16), txt[...]], axis=0)
    c3a = send(remote(gbuf.at[x, zh, c], gbuf.at[x, zh, c], c3_ss.at[0], c3_rs.at[0], c_peer))

    arrive(2, 1)
    c3a.wait_recv()
    c3b = [
        send(remote(gbuf.at[x, zh], gbuf.at[x, zh], c3_ss.at[k], c3_rs.at[k], x_peer(k))) for k in range(1, NX)
    ]
    pair(1)

    arrive(3, 0)
    for copy in c3b:
        copy.wait_recv()
    c3c = [
        send(remote(gbuf.at[:, zh], gbuf.at[:, zh], c3_ss.at[3 + k], c3_rs.at[3 + k], h_peer(k)))
        for k in range(1, NZH)
    ]
    pair(2)

    arrive(3, 1)
    pair(3)
    for copy in c3c:
        copy.wait_recv()
    every = gbuf[...].reshape(512 // 16, 32, HD)
    all_img = every[:, :16].reshape(512, HD)
    all_txt = every[:, 16:].reshape(512, HD)
    own = gbuf[x, zh, c]
    dots_img = nt(own[:16], all_txt)
    dots_txt = nt(own[16:], all_img)
    ones = jnp.ones((8, HD), F32)

    def squares(rows_):
        wide = rows_.astype(F32)
        return lax.dot_general(
            ones, wide * wide, (((1,), (1,)), ((), ())),
            preferred_element_type=F32, precision=lax.Precision.HIGHEST,
        )

    sq_img, sq_txt = squares(all_img), squares(all_txt)
    for k in range(NY):
        pk[k, 0:2] = dots_img[2 * k : 2 * k + 2]
        pk[k, 2:4] = dots_txt[2 * k : 2 * k + 2]
        pk[k, 4:6] = sq_img[4:6]
        pk[k, 6:8] = sq_txt[6:8]
    c4 = send(remote(pk, pz, c4_ss, c4_rs, z_peer))

    arrive(4, 0)
    arrive(4, 1)
    tokens = ring[6]
    grad_k, grad_v = attend(1, [y_at(4)], tokens)

    XR, HR, CR = DI // NX, DI // (NX * NZH), DI // (NX * NZH * NC)
    theirs = jnp.where(c == 0, grad_v.astype(F32), grad_k.astype(F32)).astype(BF16)
    ours = jnp.where(c == 0, grad_k.astype(F32), grad_v.astype(F32)).astype(BF16)
    t1 = []
    for i, (lo, hi) in enumerate(((0, 512), (512, 1024), (1024, DI))):
        s1[lo:hi] = (acc[1 - c, lo:hi] + tn(tokens[:, lo:hi], theirs)).astype(BF16)
        t1.append(send(remote(s1.at[lo:hi], r1.at[lo:hi], t1_ss.at[i], t1_rs.at[i], c_peer)))
    acc[c] += tn(tokens, ours)
    back = [
        send(remote(att_s, att_r, z_ss.at[2], z_rs.at[2], z_peer)),
        send(remote(gq_s, gq_r, z_ss.at[3], z_rs.at[3], z_peer)),
    ]
    c4.wait_recv()
    for k in range(NY):
        pk2[k] = pk[k] + pz[k]
    c5 = [
        send(remote(pk2.at[y_at(k)], rk.at[k], c5_ss.at[k], c5_rs.at[k], y_peer(k))) for k in range(1, NY)
    ]

    def block(k):
        return pl.ds(pl.multiple_of(x_at(k) * XR, 32), XR)

    def over_z(k):
        return remote(s2.at[k], r2.at[k], t2_ss.at[k], t2_rs.at[k], z_peer)

    def over_x(k):
        return remote(s3.at[k], r3.at[k], t3_ss.at[k], t3_rs.at[k], x_peer(k))

    def over_x2(k):
        return remote(s3w.at[k], r3w.at[k], t3_ss.at[k], t3_rs.at[k], x_peer(k))

    order = (2, 1, 3)
    for copy in t1:
        copy.wait_recv()

    @pl.when(c == 0)
    def _():
        for k in order + (0,):
            both = acc[0, block(k), :] + r1[block(k), :].astype(F32)
            own2[k] = both[:, :HD]
            s2[k] = both[:, HD:].astype(BF16)
            over_z(k).start()

    @pl.when(c == 1)
    def _():
        for k in order:
            s3w[k] = (acc[1, block(k), :] + r1[block(k), :].astype(F32)).astype(BF16)
            over_x2(k).start()
        own_w[...] = acc[1, block(0), :] + r1[block(0), :].astype(F32)

    total = pk2[y]
    for k in range(1, NY):
        c5[k - 1].wait_recv()
        total += rk[k]
    spot = lax.broadcasted_iota(jnp.int32, (2, 512), 1)
    index = d * 16 + 2 * y + lax.broadcasted_iota(jnp.int32, (2, 512), 0)
    hit = spot == index
    sq_i, sq_t = total[4:5], total[6:7]

    def side(dots, sq_rows, sq_cols):
        sq_row = jnp.sum(jnp.where(hit, sq_rows, 0.0), axis=1, keepdims=True)
        logits = temp[0] * dots * lax.rsqrt(sq_row + 1e-6) * lax.rsqrt(sq_cols + 1e-6)
        top = jnp.max(logits, axis=1, keepdims=True)
        lse = top + jnp.log(jnp.sum(jnp.exp(logits - top), axis=1, keepdims=True))
        return lse - jnp.sum(jnp.where(hit, logits, 0.0), axis=1, keepdims=True)

    img_side = side(total[0:2], sq_i, sq_t)
    txt_side = side(total[2:4], sq_t, sq_i)
    lane = lax.broadcasted_iota(jnp.int32, (8, 128), 1)
    line = lax.broadcasted_iota(jnp.int32, (8, 128), 0)
    tile = jnp.zeros((8, 128), F32)
    for r in range(2):
        here_lane = lane == 2 * y + r
        tile = jnp.where(here_lane & (line == 0), img_side[r : r + 1], tile)
        tile = jnp.where(here_lane & (line == 1), txt_side[r : r + 1], tile)
    cs[...] = tile
    c6 = [send(remote(cs, cr.at[k], c6_ss.at[k], c6_rs.at[k], y_peer(k))) for k in range(1, NY)]

    @pl.when(c == 0)
    def _():
        for k in order:
            over_z(k).wait_recv()
            s3[k] = (own2[k] + r2[k].astype(F32)).astype(BF16)
            over_x(k).start()
        over_z(0).wait_recv()
        block_sum = own2[0] + r2[0].astype(F32)
        for k in order:
            over_x(k).wait_recv()
            block_sum += r3[k].astype(F32)
        t3[...] = block_sum

    @pl.when(c == 1)
    def _():
        for k in order:
            over_x2(k).wait_recv()
        wide = own_w[...]
        for k in order:
            wide += r3w[k].astype(F32)
        s2[0] = wide[:, HD:].astype(BF16)
        over_z(0).start()
        over_z(0).wait_recv()
        t3[...] = wide[:, :HD] + r2[0].astype(F32)

    t4 = []
    for k in range(1, NZH):
        s4[k, 0:HR] = t3[pl.ds(pl.multiple_of(h_at(k) * HR, 8), HR), :].astype(BF16)
        t4.append(send(remote(s4.at[k], r4.at[k], t4_ss.at[k], t4_rs.at[k], h_peer(k))))
    piece = t3[pl.ds(pl.multiple_of(zh * HR, 8), HR), :]
    for copy in back:
        copy.wait_recv()
    att[away] = att_r[...]
    gq[away] = gq_r[...]
    answer = cs[...]
    for k in range(1, NY):
        c6[k - 1].wait_recv()
        answer += cr[k]
    con[...] = answer[0:2, 0:16]
    for k in range(1, NZH):
        t4[k - 1].wait_recv()
        piece += r4[k, 0:HR].astype(F32)
    low, high = piece[:CR], piece[CR:]
    s5[0:CR] = jnp.where(c == 0, high, low)
    t5 = send(remote(s5, r5, t5_ss, t5_rs, c_peer))
    kept = jnp.where(c == 0, low, high)

    for copy in sent:
        if copy is not t5:
            copy.wait_send()

    @pl.when(c == 0)
    def _():
        for k in order + (0,):
            over_z(k).wait_send()
        for k in order:
            over_x(k).wait_send()

    @pl.when(c == 1)
    def _():
        for k in order:
            over_x2(k).wait_send()
        over_z(0).wait_send()

    t5.wait_recv()
    got = r5[0:CR]
    dwk[...] = jnp.where(c == 0, kept, got)
    dwv[...] = jnp.where(c == 0, got, kept)
    t5.wait_send()


def body(img_tokens, w_key, w_value, queries, lengths, d_out, img_pooled, w_proj, txt_embed, inv_temp):
    vmem = pl.BlockSpec(memory_space=pltpu.VMEM)
    smem = pl.BlockSpec(memory_space=pltpu.SMEM)
    hbm = pl.BlockSpec(memory_space=pltpu.HBM)
    dma = pltpu.SemaphoreType.DMA
    V = pltpu.VMEM
    return pl.pallas_call(
        kernel,
        out_shape=(
            jax.ShapeDtypeStruct((16, 32, HD), BF16),
            jax.ShapeDtypeStruct((16, 32, HD), BF16),
            jax.ShapeDtypeStruct((44, HD), F32),
            jax.ShapeDtypeStruct((44, HD), F32),
            jax.ShapeDtypeStruct((2, 16), F32),
        ),
        in_specs=[hbm] * 9 + [smem],
        out_specs=(vmem,) * 5,
        scratch_shapes=[
            V((128, DI), BF16),
            V((16, 32, HD), BF16),
            pltpu.SMEM((16,), jnp.int32),
            V((16, 32, HD), BF16),
            V((1, DI), BF16),
            V((DI, HD), BF16),
            V((16, HD), BF16),
            dma((9,)),
            V((7, 128, DI), BF16),
            V((2, DI, 256), BF16),
            V((8, 32, HD), BF16),
            V((8, 32, HD), BF16),
            V((8, 32, HD), BF16),
            V((8, 32, HD), BF16),
            V((8, 32, HD), BF16),
            V((8, 32, HD), BF16),
            V((2, DI, 256), F32),
            V((DI, 256), BF16),
            V((DI, 256), BF16),
            V((4, 352, HD), F32),
            V((4, 352, HD), BF16),
            V((4, 352, HD), BF16),
            V((4, 352, HD), BF16),
            V((4, 352, HD), BF16),
            V((352, 256), F32),
            V((4, 352, 256), BF16),
            V((4, 352, 256), BF16),
            V((352, HD), F32),
            V((4, 96, HD), BF16),
            V((4, 96, HD), BF16),
            V((48, HD), F32),
            V((48, HD), F32),
            V((2, 8, 16, 128), F32),
            V((4, 4, 2, 32, HD), BF16),
            V((8, 8, 512), F32),
            V((8, 8, 512), F32),
            V((8, 8, 512), F32),
            V((8, 8, 512), F32),
            V((8, 128), F32),
            V((8, 8, 128), F32),
            dma((2, 4, 2)), dma((2, 4, 2)),
            dma((4,)), dma((4,)),
            dma((2,)), dma((2,)),
            dma((8,)), dma((8,)),
            dma, dma,
            dma((7,)), dma((7,)),
            dma, dma,
            dma((8,)), dma((8,)),
            dma((8,)), dma((8,)),
            dma((3,)), dma((3,)),
            dma((4,)), dma((4,)),
            dma((4,)), dma((4,)),
            dma((4,)), dma((4,)),
            dma, dma,
        ],
        compiler_params=pltpu.CompilerParams(
            collective_id=0, has_side_effects=True, vmem_limit_bytes=60 * 1024 * 1024
        ),
        cost_estimate=pl.CostEstimate(flops=6_200_000_000, bytes_accessed=4_000_000, transcendentals=100_000),
    )(
        img_tokens.reshape(128, DI), w_key, w_value, queries, lengths, d_out, img_pooled, w_proj, txt_embed, inv_temp
    )


def solution(mesh):
    placed = (
        P(("dp", "mp"), None, None),
        P(None, "mp"),
        P(None, "mp"),
        P("dp", None, "mp"),
        P("dp"),
        P("dp", None, "mp"),
        P(("dp", "mp"), None),
        P(None, "mp"),
        P("dp", "mp"),
        P(),
    )
    return jax.shard_map(
        body,
        mesh=mesh,
        in_specs=placed,
        out_specs=(
            P("dp", None, "mp"),
            P("dp", None, "mp"),
            P("dp", "mp"),
            P("dp", "mp"),
            P(None, "dp"),
        ),
        check_vma=False,
    )
```

```python
import functools

import jax
import jax.numpy as jnp
from jax import lax
from jax.experimental import pallas as pl
from jax.experimental.pallas import tpu as pltpu
from jax.sharding import PartitionSpec as P

HD = 128
NX, NZH, NC, NZL, NY = 4, 4, 2, 2, 8
DI = 1408
ROOT = HD ** (-0.5)
MESH = pl.DeviceIdType.MESH
F32 = jnp.float32
BF16 = jnp.bfloat16


def nt(a, b):
    return lax.dot_general(a, b, (((1,), (1,)), ((), ())), preferred_element_type=F32)


def tn(a, b):
    return lax.dot_general(a, b, (((0,), (0,)), ((), ())), preferred_element_type=F32)


def nn(a, b):
    return jnp.dot(a, b, preferred_element_type=F32)


def kernel(
    tok_in, wk, wv, q_in, length_in, do_in, pooled_in, wp_in, txt_in, temp,
    ag, dw, con,
    tok, q, length, do, pooled, wp, txt, in_sem,
    ring, w, qp, dop, out_s, out_r, acc, mine,
    s1, r1, own2, s2, r2, s3, r3, own_w, s3w, r3w, t3, s4, r4, s5, r5,
    prow, pwide, gbuf, pk, pz, pk2, rk, cs, cr,
    ring_ss, ring_rs, z_ss, z_rs, w_ss, w_rs, c1_ss, c1_rs, c2_ss, c2_rs, c3_ss, c3_rs,
    c4_ss, c4_rs, c5_ss, c5_rs, c6_ss, c6_rs, t1_ss, t1_rs, t2_ss, t2_rs, t3_ss, t3_rs,
    t4_ss, t4_rs, t5_ss, t5_rs,
):
    att, gq, dwk, dwv = ag.at[0], ag.at[1], dw.at[0], dw.at[1]
    d = lax.axis_index("dp")
    m = lax.axis_index("mp")
    x, zh, c = d // (NZH * NC), lax.rem(d // NC, NZH), lax.rem(d, NC)
    zl, y = m // NY, lax.rem(m, NY)

    def y_at(k):
        return lax.rem(y + k + NY, NY)

    def y_peer(k):
        return (d, zl * NY + y_at(k))

    def x_at(k):
        return lax.rem(x + k, NX)

    def x_peer(k):
        return (x_at(k) * (NZH * NC) + zh * NC + c, m)

    def h_at(k):
        return lax.rem(zh + k, NZH)

    def h_peer(k):
        return (x * (NZH * NC) + h_at(k) * NC + c, m)

    z_peer = (d, (1 - zl) * NY + y)
    c_peer = (d + 1 - 2 * c, m)

    def remote(src, dst, ss, rs, to):
        return pltpu.make_async_remote_copy(
            src_ref=src, dst_ref=dst, send_sem=ss, recv_sem=rs, device_id=to, device_id_type=MESH
        )

    sent = []

    def send(copy):
        copy.start()
        sent.append(copy)
        return copy

    loads = [
        pltpu.make_async_copy(src, dst, in_sem.at[i])
        for i, (src, dst) in enumerate(
            (
                (wk, w.at[0, :, pl.ds(0, HD)]), (wv, w.at[0, :, pl.ds(HD, HD)]), (pooled_in, pooled),
                (tok_in, tok), (q_in, q), (do_in, do), (wp_in, wp), (txt_in, txt), (length_in, length),
            )
        )
    ]
    for copy in loads:
        copy.start()

    barrier = pltpu.get_barrier_semaphore()
    peers = [y_peer(k) for k in range(1, NY)] + [z_peer, c_peer]
    peers += [x_peer(k) for k in range(1, NX)] + [h_peer(k) for k in range(1, NZH)]
    for peer in peers:
        pl.semaphore_signal(barrier, inc=1, device_id=peer, device_id_type=MESH)

    for copy in loads:
        copy.wait()
    row = jnp.zeros((16, 128), F32)
    rows = lax.broadcasted_iota(jnp.int32, (16, 128), 0)
    for i in range(DI // 128):
        piece = pooled[0:1, i * 128 : (i + 1) * 128].astype(F32)
        row = jnp.where(rows == i, piece, row)
    prow[zl, y] = row.astype(BF16)
    s4[...] = jnp.zeros_like(s4)
    s5[...] = jnp.zeros_like(s5)

    pl.semaphore_wait(barrier, len(peers))

    def hop(way, dist, half):
        side = 0 if way > 0 else 1
        part = pl.ds(half * 64, 64)
        src = tok_in.at[part] if dist == 1 else ring.at[2 * (dist - 2) + side, part]
        slot = 6 if dist == 4 else 2 * (dist - 1) + side
        return remote(
            src, ring.at[slot, part], ring_ss.at[side, dist - 1, half], ring_rs.at[side, dist - 1, half],
            y_peer(way),
        )

    def arrive(dist, half):
        for way in (1, -1):
            if dist < 4 or (half == 0) == (way > 0):
                hop(way, dist, half).wait_recv()
                if dist < 3 or (dist == 3 and (half == 0) == (way > 0)):
                    send(hop(way, dist + 1, half))

    for way in (1, -1):
        send(hop(way, 1, 0))
    c1 = [send(remote(prow.at[zl, y], prow.at[zl, y], c1_ss.at[k], c1_rs.at[k], y_peer(k))) for k in range(1, NY)]
    for way in (1, -1):
        send(hop(way, 1, 1))
    away = pl.ds((1 - zl) * NY, NY)
    cols = pl.ds(pl.multiple_of(c * HD, HD), HD)
    cols_there = pl.ds(pl.multiple_of((1 - c) * HD, HD), HD)
    swap_w = send(remote(w.at[0, :, cols], w.at[1, :, cols], w_ss.at[0], w_rs.at[0], z_peer))
    swap_q = send(remote(q_in.at[away], qp, z_ss.at[0], z_rs.at[0], z_peer))
    swap_do = send(remote(do_in.at[away], dop, z_ss.at[1], z_rs.at[1], z_peer))
    spots = lax.broadcasted_iota(jnp.int32, (32, 128), 0)

    def attend(heads, sources, tokens, first):
        items = [(h, i) for h in heads for i in range(len(sources))]
        pairs = {h: nn(tokens, w[h]).astype(BF16) for h in heads}
        keys = [pairs[h][i * 128 : (i + 1) * 128, :HD] for h, i in items]
        values = [pairs[h][i * 128 : (i + 1) * 128, HD:] for h, i in items]
        keeps = [spots < length[zl * NY + src] for src in sources]
        query, masked = [], []
        for h, i in items:
            src = sources[i]
            query.append(q[zl * NY + src] if h == 0 else qp[src])
            cot = do[zl * NY + src] if h == 0 else dop[src]
            masked.append(jnp.where(keeps[i], cot.astype(F32), 0.0).astype(BF16))
        scores = jnp.concatenate([nt(a, b) for a, b in zip(query, keys)], axis=0) * ROOT
        grad_probs = jnp.concatenate([nt(a, b) for a, b in zip(masked, values)], axis=0)
        top = jnp.max(scores, axis=1, keepdims=True)
        e = jnp.exp(scores - top)
        probs = e / jnp.sum(e, axis=1, keepdims=True)
        probs_b = probs.astype(BF16)
        dots = jnp.sum(probs * grad_probs, axis=1, keepdims=True)
        grad_scores = (probs * (grad_probs - dots) * ROOT).astype(BF16)

        def rows_of(a, n):
            return a[n * 32 : (n + 1) * 32]

        outs = [nn(rows_of(probs_b, n), values[n]) for n in range(len(items))]
        grad_v = [tn(rows_of(probs_b, n), masked[n]).astype(BF16) for n in range(len(items))]
        grad_q = [nn(rows_of(grad_scores, n), keys[n]).astype(BF16) for n in range(len(items))]
        grad_k = [tn(rows_of(grad_scores, n), query[n]).astype(BF16) for n in range(len(items))]
        for n, (h, i) in enumerate(items):
            out = jnp.where(keeps[i], outs[n], 0.0).astype(BF16)
            if h == 0:
                att[zl * NY + sources[i]] = out
                gq[zl * NY + sources[i]] = grad_q[n]
            else:
                out_s[first + i, 0] = out
                out_s[first + i, 1] = grad_q[n]
        both = [jnp.concatenate([grad_k[n], grad_v[n]], axis=1) for n in range(len(items))]
        count = len(sources)
        grads = [both[n * count : (n + 1) * count] for n in range(len(heads))]
        return [g[0] if count == 1 else jnp.concatenate(g, axis=0) for g in grads]

    def pair_tokens(dist):
        lo = 2 * (dist - 1)
        return ring[lo : lo + 2].reshape(256, DI)

    def pair(dist, heads):
        tokens = pair_tokens(dist)
        grads = attend(heads, [y_at(-dist), y_at(dist)], tokens, 2 * dist - 1)
        if len(heads) == 1:
            acc[heads[0]] += tn(tokens, grads[0])
        else:
            term = tn(tokens, jnp.concatenate(grads, axis=1))
            acc[0] += term[:, :256]
            acc[1] += term[:, 256:]

    acc[0] = tn(tok[...], attend((0,), [y], tok[...], 0)[0])

    arrive(1, 0)
    for copy in c1:
        copy.wait_recv()
    c2 = send(remote(prow.at[zl], prow.at[zl], c2_ss, c2_rs, z_peer))
    arrive(1, 1)
    swap_w.wait_recv()
    share_w = send(remote(w.at[1, :, cols], w.at[1, :, cols], w_ss.at[1], w_rs.at[1], c_peer))
    pair(1, (0,))

    arrive(2, 0)
    c2.wait_recv()
    pwide[...] = prow[...].reshape(16, 16, 128).astype(F32)
    part = jnp.zeros((16, HD), F32)
    for i in range(DI // 128):
        part += nn(pwide[:, i, :].astype(BF16), wp[i * 128 : (i + 1) * 128, :])
    gbuf[x, zh, c] = jnp.concatenate([part.astype(BF16), txt[...]], axis=0)
    c3a = send(remote(gbuf.at[x, zh, c], gbuf.at[x, zh, c], c3_ss.at[0], c3_rs.at[0], c_peer))
    swap_q.wait_recv()
    swap_do.wait_recv()
    share_w.wait_recv()
    acc[1] = tn(tok[...], attend((1,), [y], tok[...], 0)[0])
    pair(1, (1,))

    arrive(2, 1)
    c3a.wait_recv()
    c3b = [
        send(remote(gbuf.at[x, zh], gbuf.at[x, zh], c3_ss.at[k], c3_rs.at[k], x_peer(k))) for k in range(1, NX)
    ]
    pair(2, (0, 1))

    arrive(3, 0)
    for copy in c3b:
        copy.wait_recv()
    c3c = [
        send(remote(gbuf.at[:, zh], gbuf.at[:, zh], c3_ss.at[3 + k], c3_rs.at[3 + k], h_peer(k)))
        for k in range(1, NZH)
    ]

    arrive(3, 1)
    pair(3, (0, 1))
    back = [send(remote(out_s.at[0:7], out_r.at[0:7], z_ss.at[2], z_rs.at[2], z_peer))]
    for copy in c3c:
        copy.wait_recv()
    every = gbuf[...].reshape(512 // 16, 32, HD)
    all_img = every[:, :16].reshape(512, HD)
    all_txt = every[:, 16:].reshape(512, HD)
    own = gbuf[x, zh, c]
    dots_img = nt(own[:16], all_txt)
    dots_txt = nt(own[16:], all_img)
    ones = jnp.ones((8, HD), F32)

    def squares(rows_):
        wide = rows_.astype(F32)
        return lax.dot_general(
            ones, wide * wide, (((1,), (1,)), ((), ())),
            preferred_element_type=F32, precision=lax.Precision.HIGHEST,
        )

    sq_img, sq_txt = squares(all_img), squares(all_txt)
    for k in range(NY):
        pk[k, 0:2] = dots_img[2 * k : 2 * k + 2]
        pk[k, 2:4] = dots_txt[2 * k : 2 * k + 2]
        pk[k, 4:6] = sq_img[4:6]
        pk[k, 6:8] = sq_txt[6:8]
    c4 = send(remote(pk, pz, c4_ss, c4_rs, z_peer))

    arrive(4, 0)
    arrive(4, 1)
    tokens = ring[6]
    grads = attend((0, 1), [y_at(4)], tokens, 7)

    XR, HR, CR = DI // NX, DI // (NX * NZH), DI // (NX * NZH * NC)
    keys_part = jnp.concatenate([g[:, :HD] for g in grads], axis=1).astype(F32)
    values_part = jnp.concatenate([g[:, HD:] for g in grads], axis=1).astype(F32)
    theirs = jnp.where(c == 0, values_part, keys_part).astype(BF16)
    ours = jnp.where(c == 0, keys_part, values_part).astype(BF16)
    t1 = []
    for i, (lo, hi) in enumerate(((0, 512), (512, 1024), (1024, DI))):
        term = tn(tokens[:, lo:hi], theirs)
        s1[lo:hi, :HD] = (acc[0, lo:hi, cols_there] + term[:, :HD]).astype(BF16)
        s1[lo:hi, HD:] = (acc[1, lo:hi, cols_there] + term[:, HD:]).astype(BF16)
        t1.append(send(remote(s1.at[lo:hi], r1.at[lo:hi], t1_ss.at[i], t1_rs.at[i], c_peer)))
    back.append(send(remote(out_s.at[7], out_r.at[7], z_ss.at[3], z_rs.at[3], z_peer)))
    term = tn(tokens, ours)
    mine[:, :HD] = acc[0, :, cols] + term[:, :HD]
    mine[:, HD:] = acc[1, :, cols] + term[:, HD:]
    c4.wait_recv()
    for k in range(NY):
        pk2[k] = pk[k] + pz[k]
    c5 = [
        send(remote(pk2.at[y_at(k)], rk.at[k], c5_ss.at[k], c5_rs.at[k], y_peer(k))) for k in range(1, NY)
    ]

    def block(k):
        return pl.ds(pl.multiple_of(x_at(k) * XR, 32), XR)

    def over_z(k):
        return remote(s2.at[k], r2.at[k], t2_ss.at[k], t2_rs.at[k], z_peer)

    def over_x(k):
        return remote(s3.at[k], r3.at[k], t3_ss.at[k], t3_rs.at[k], x_peer(k))

    def over_x2(k):
        return remote(s3w.at[k], r3w.at[k], t3_ss.at[k], t3_rs.at[k], x_peer(k))

    order = (2, 1, 3)
    for copy in t1:
        copy.wait_recv()

    @pl.when(c == 0)
    def _():
        for k in order + (0,):
            both = mine[block(k), :] + r1[block(k), :].astype(F32)
            own2[k] = both[:, :HD]
            s2[k] = both[:, HD:].astype(BF16)
            over_z(k).start()

    @pl.when(c == 1)
    def _():
        for k in order:
            s3w[k] = (mine[block(k), :] + r1[block(k), :].astype(F32)).astype(BF16)
            over_x2(k).start()
        own_w[...] = mine[block(0), :] + r1[block(0), :].astype(F32)

    total = pk2[y]
    for k in range(1, NY):
        c5[k - 1].wait_recv()
        total += rk[k]
    spot = lax.broadcasted_iota(jnp.int32, (2, 512), 1)
    index = d * 16 + 2 * y + lax.broadcasted_iota(jnp.int32, (2, 512), 0)
    hit = spot == index
    sq_i, sq_t = total[4:5], total[6:7]

    def side(dots, sq_rows, sq_cols):
        sq_row = jnp.sum(jnp.where(hit, sq_rows, 0.0), axis=1, keepdims=True)
        logits = temp[0] * dots * lax.rsqrt(sq_row + 1e-6) * lax.rsqrt(sq_cols + 1e-6)
        top = jnp.max(logits, axis=1, keepdims=True)
        lse = top + jnp.log(jnp.sum(jnp.exp(logits - top), axis=1, keepdims=True))
        return lse - jnp.sum(jnp.where(hit, logits, 0.0), axis=1, keepdims=True)

    img_side = side(total[0:2], sq_i, sq_t)
    txt_side = side(total[2:4], sq_t, sq_i)
    lane = lax.broadcasted_iota(jnp.int32, (8, 128), 1)
    line = lax.broadcasted_iota(jnp.int32, (8, 128), 0)
    tile = jnp.zeros((8, 128), F32)
    for r in range(2):
        here_lane = lane == 2 * y + r
        tile = jnp.where(here_lane & (line == 0), img_side[r : r + 1], tile)
        tile = jnp.where(here_lane & (line == 1), txt_side[r : r + 1], tile)
    cs[...] = tile
    c6 = [send(remote(cs, cr.at[k], c6_ss.at[k], c6_rs.at[k], y_peer(k))) for k in range(1, NY)]

    @pl.when(c == 0)
    def _():
        for k in order:
            over_z(k).wait_recv()
            s3[k] = (own2[k] + r2[k].astype(F32)).astype(BF16)
            over_x(k).start()
        over_z(0).wait_recv()
        block_sum = own2[0] + r2[0].astype(F32)
        for k in order:
            over_x(k).wait_recv()
            block_sum += r3[k].astype(F32)
        t3[...] = block_sum

    @pl.when(c == 1)
    def _():
        for k in order:
            over_x2(k).wait_recv()
        wide = own_w[...]
        for k in order:
            wide += r3w[k].astype(F32)
        s2[0] = wide[:, HD:].astype(BF16)
        over_z(0).start()
        over_z(0).wait_recv()
        t3[...] = wide[:, :HD] + r2[0].astype(F32)

    t4 = []
    for k in range(1, NZH):
        s4[k, 0:HR] = t3[pl.ds(pl.multiple_of(h_at(k) * HR, 8), HR), :].astype(BF16)
        t4.append(send(remote(s4.at[k], r4.at[k], t4_ss.at[k], t4_rs.at[k], h_peer(k))))
    piece = t3[pl.ds(pl.multiple_of(zh * HR, 8), HR), :]
    for copy in back:
        copy.wait_recv()
    for i, dist in enumerate((0, -1, 1, -2, 2, -3, 3, 4)):
        att[(1 - zl) * NY + y_at(dist)] = out_r[i, 0]
        gq[(1 - zl) * NY + y_at(dist)] = out_r[i, 1]
    answer = cs[...]
    for k in range(1, NY):
        c6[k - 1].wait_recv()
        answer += cr[k]
    con[...] = answer[0:2, 0:16]
    for k in range(1, NZH):
        t4[k - 1].wait_recv()
        piece += r4[k, 0:HR].astype(F32)
    low, high = piece[:CR], piece[CR:]
    s5[0:CR] = jnp.where(c == 0, high, low)
    t5 = send(remote(s5, r5, t5_ss, t5_rs, c_peer))
    kept = jnp.where(c == 0, low, high)

    for copy in sent:
        if copy is not t5:
            copy.wait_send()

    @pl.when(c == 0)
    def _():
        for k in order + (0,):
            over_z(k).wait_send()
        for k in order:
            over_x(k).wait_send()

    @pl.when(c == 1)
    def _():
        for k in order:
            over_x2(k).wait_send()
        over_z(0).wait_send()

    t5.wait_recv()
    got = r5[0:CR]
    dwk[...] = jnp.where(c == 0, kept, got)
    dwv[...] = jnp.where(c == 0, got, kept)
    t5.wait_send()


def body(img_tokens, w_key, w_value, queries, lengths, d_out, img_pooled, w_proj, txt_embed, inv_temp):
    vmem = pl.BlockSpec(memory_space=pltpu.VMEM)
    smem = pl.BlockSpec(memory_space=pltpu.SMEM)
    hbm = pl.BlockSpec(memory_space=pltpu.HBM)
    dma = pltpu.SemaphoreType.DMA
    V = pltpu.VMEM
    ag, dw, con = pl.pallas_call(
        kernel,
        out_shape=(
            jax.ShapeDtypeStruct((2, 16, 32, HD), BF16),
            jax.ShapeDtypeStruct((2, 44, HD), F32),
            jax.ShapeDtypeStruct((2, 16), F32),
        ),
        in_specs=[hbm] * 9 + [smem],
        out_specs=(vmem,) * 3,
        scratch_shapes=[
            V((128, DI), BF16),
            V((16, 32, HD), BF16),
            pltpu.SMEM((16,), jnp.int32),
            V((16, 32, HD), BF16),
            V((1, DI), BF16),
            V((DI, HD), BF16),
            V((16, HD), BF16),
            dma((9,)),
            V((7, 128, DI), BF16),
            V((2, DI, 256), BF16),
            V((8, 32, HD), BF16),
            V((8, 32, HD), BF16),
            V((8, 2, 32, HD), BF16),
            V((8, 2, 32, HD), BF16),
            V((2, DI, 256), F32),
            V((DI, 256), F32),
            V((DI, 256), BF16),
            V((DI, 256), BF16),
            V((4, 352, HD), F32),
            V((4, 352, HD), BF16),
            V((4, 352, HD), BF16),
            V((4, 352, HD), BF16),
            V((4, 352, HD), BF16),
            V((352, 256), F32),
            V((4, 352, 256), BF16),
            V((4, 352, 256), BF16),
            V((352, HD), F32),
            V((4, 96, HD), BF16),
            V((4, 96, HD), BF16),
            V((48, HD), F32),
            V((48, HD), F32),
            V((2, 8, 16, 128), BF16),
            V((16, 16, 128), F32),
            V((4, 4, 2, 32, HD), BF16),
            V((8, 8, 512), F32),
            V((8, 8, 512), F32),
            V((8, 8, 512), F32),
            V((8, 8, 512), F32),
            V((8, 128), F32),
            V((8, 8, 128), F32),
            dma((2, 4, 2)), dma((2, 4, 2)),
            dma((4,)), dma((4,)),
            dma((2,)), dma((2,)),
            dma((8,)), dma((8,)),
            dma, dma,
            dma((7,)), dma((7,)),
            dma, dma,
            dma((8,)), dma((8,)),
            dma((8,)), dma((8,)),
            dma((3,)), dma((3,)),
            dma((4,)), dma((4,)),
            dma((4,)), dma((4,)),
            dma((4,)), dma((4,)),
            dma, dma,
        ],
        compiler_params=pltpu.CompilerParams(
            collective_id=0, has_side_effects=True, vmem_limit_bytes=60 * 1024 * 1024
        ),
        cost_estimate=pl.CostEstimate(flops=6_200_000_000, bytes_accessed=4_000_000, transcendentals=100_000),
    )(
        img_tokens.reshape(128, DI), w_key, w_value, queries, lengths, d_out, img_pooled, w_proj, txt_embed, inv_temp
    )
    return ag[0], ag[1], dw[0], dw[1], con


def solution(mesh):
    placed = (
        P(("dp", "mp"), None, None),
        P(None, "mp"),
        P(None, "mp"),
        P("dp", None, "mp"),
        P("dp"),
        P("dp", None, "mp"),
        P(("dp", "mp"), None),
        P(None, "mp"),
        P("dp", "mp"),
        P(),
    )
    return jax.shard_map(
        body,
        mesh=mesh,
        in_specs=placed,
        out_specs=(
            P("dp", None, "mp"),
            P("dp", None, "mp"),
            P("dp", "mp"),
            P("dp", "mp"),
            P(None, "dp"),
        ),
        check_vma=False,
    )
```

```python
import functools

import jax
import jax.numpy as jnp
from jax import lax
from jax.experimental import pallas as pl
from jax.experimental.pallas import tpu as pltpu
from jax.sharding import PartitionSpec as P

HD = 128
NX, NZH, NC, NZL, NY = 4, 4, 2, 2, 8
DI = 1408
ROOT = HD ** (-0.5)
MESH = pl.DeviceIdType.MESH
F32 = jnp.float32
BF16 = jnp.bfloat16


def nt(a, b):
    return lax.dot_general(a, b, (((1,), (1,)), ((), ())), preferred_element_type=F32)


def tn(a, b):
    return lax.dot_general(a, b, (((0,), (0,)), ((), ())), preferred_element_type=F32)


def nn(a, b):
    return jnp.dot(a, b, preferred_element_type=F32)


def kernel(
    tok_in, wk, wv, q_in, length_in, do_in, pooled_in, wp_in, txt_in, temp,
    ag, dw, con,
    tok, q, length, do, pooled, wp, txt, in_sem,
    ring, w, qp, dop, out_s, out_r, acc, mine,
    s1, r1, own2, s2, r2, s3, r3, own_w, s3w, r3w, t3, s4, r4, s5, r5,
    prow, pwide, gbuf, pk, pz, pk2, rk, cs, cr,
    ring_ss, ring_rs, z_ss, z_rs, w_ss, w_rs, c1_ss, c1_rs, c2_ss, c2_rs, c3_ss, c3_rs,
    c4_ss, c4_rs, c5_ss, c5_rs, c6_ss, c6_rs, t1_ss, t1_rs, t2_ss, t2_rs, t3_ss, t3_rs,
    t4_ss, t4_rs, t5_ss, t5_rs,
):
    att, gq, dwk, dwv = ag.at[0], ag.at[1], dw.at[0], dw.at[1]
    d = lax.axis_index("dp")
    m = lax.axis_index("mp")
    x, zh, c = d // (NZH * NC), lax.rem(d // NC, NZH), lax.rem(d, NC)
    zl, y = m // NY, lax.rem(m, NY)

    def y_at(k):
        return lax.rem(y + k + NY, NY)

    def y_peer(k):
        return (d, zl * NY + y_at(k))

    def x_at(k):
        return lax.rem(x + k, NX)

    def x_peer(k):
        return (x_at(k) * (NZH * NC) + zh * NC + c, m)

    def h_at(k):
        return lax.rem(zh + k, NZH)

    def h_peer(k):
        return (x * (NZH * NC) + h_at(k) * NC + c, m)

    z_peer = (d, (1 - zl) * NY + y)
    c_peer = (d + 1 - 2 * c, m)

    def remote(src, dst, ss, rs, to):
        return pltpu.make_async_remote_copy(
            src_ref=src, dst_ref=dst, send_sem=ss, recv_sem=rs, device_id=to, device_id_type=MESH
        )

    sent = []

    def send(copy):
        copy.start()
        sent.append(copy)
        return copy

    loads = [
        pltpu.make_async_copy(src, dst, in_sem.at[i])
        for i, (src, dst) in enumerate(
            (
                (wk, w.at[0, :, pl.ds(0, HD)]), (wv, w.at[0, :, pl.ds(HD, HD)]), (pooled_in, pooled),
                (tok_in, tok), (q_in, q), (do_in, do), (wp_in, wp), (txt_in, txt), (length_in, length),
            )
        )
    ]
    for copy in loads:
        copy.start()

    barrier = pltpu.get_barrier_semaphore()
    peers = [y_peer(k) for k in range(1, NY)] + [z_peer, c_peer]
    peers += [x_peer(k) for k in range(1, NX)] + [h_peer(k) for k in range(1, NZH)]
    for peer in peers:
        pl.semaphore_signal(barrier, inc=1, device_id=peer, device_id_type=MESH)

    for copy in loads:
        copy.wait()
    row = jnp.zeros((16, 128), F32)
    rows = lax.broadcasted_iota(jnp.int32, (16, 128), 0)
    for i in range(DI // 128):
        piece = pooled[0:1, i * 128 : (i + 1) * 128].astype(F32)
        row = jnp.where(rows == i, piece, row)
    prow[zl, y] = row.astype(BF16)
    s4[...] = jnp.zeros_like(s4)
    s5[...] = jnp.zeros_like(s5)

    pl.semaphore_wait(barrier, len(peers))

    def hop(way, dist, half):
        side = 0 if way > 0 else 1
        part = pl.ds(half * 64, 64)
        src = tok_in.at[part] if dist == 1 else ring.at[2 * (dist - 2) + side, part]
        slot = 6 if dist == 4 else 2 * (dist - 1) + side
        return remote(
            src, ring.at[slot, part], ring_ss.at[side, dist - 1, half], ring_rs.at[side, dist - 1, half],
            y_peer(way),
        )

    def arrive(dist, half):
        for way in (-1, 1):
            if dist < 4 or (half == 0) == (way > 0):
                hop(way, dist, half).wait_recv()
                if dist < 3 or (dist == 3 and (half == 0) == (way > 0)):
                    send(hop(way, dist + 1, half))

    for way in (1, -1):
        send(hop(way, 1, 0))
    c1 = [send(remote(prow.at[zl, y], prow.at[zl, y], c1_ss.at[k], c1_rs.at[k], y_peer(k))) for k in range(1, NY)]
    for way in (1, -1):
        send(hop(way, 1, 1))
    away = pl.ds((1 - zl) * NY, NY)
    cols = pl.ds(pl.multiple_of(c * HD, HD), HD)
    cols_there = pl.ds(pl.multiple_of((1 - c) * HD, HD), HD)
    swap_w = send(remote(w.at[0, :, cols], w.at[1, :, cols], w_ss.at[0], w_rs.at[0], z_peer))
    swap_q = send(remote(q_in.at[away], qp, z_ss.at[0], z_rs.at[0], z_peer))
    swap_do = send(remote(do_in.at[away], dop, z_ss.at[1], z_rs.at[1], z_peer))
    spots = lax.broadcasted_iota(jnp.int32, (32, 128), 0)

    def attend(heads, sources, tokens, first):
        items = [(h, i) for h in heads for i in range(len(sources))]
        pairs = {h: nn(tokens, w[h]).astype(BF16) for h in heads}
        keys = [pairs[h][i * 128 : (i + 1) * 128, :HD] for h, i in items]
        values = [pairs[h][i * 128 : (i + 1) * 128, HD:] for h, i in items]
        keeps = [spots < length[zl * NY + src] for src in sources]
        query, masked = [], []
        for h, i in items:
            src = sources[i]
            query.append(q[zl * NY + src] if h == 0 else qp[src])
            cot = do[zl * NY + src] if h == 0 else dop[src]
            masked.append(jnp.where(keeps[i], cot.astype(F32), 0.0).astype(BF16))
        scores = jnp.concatenate([nt(a, b) for a, b in zip(query, keys)], axis=0) * ROOT
        grad_probs = jnp.concatenate([nt(a, b) for a, b in zip(masked, values)], axis=0)
        top = jnp.max(scores, axis=1, keepdims=True)
        e = jnp.exp(scores - top)
        probs = e / jnp.sum(e, axis=1, keepdims=True)
        probs_b = probs.astype(BF16)
        dots = jnp.sum(probs * grad_probs, axis=1, keepdims=True)
        grad_scores = (probs * (grad_probs - dots) * ROOT).astype(BF16)

        def rows_of(a, n):
            return a[n * 32 : (n + 1) * 32]

        outs = [nn(rows_of(probs_b, n), values[n]) for n in range(len(items))]
        grad_v = [tn(rows_of(probs_b, n), masked[n]).astype(BF16) for n in range(len(items))]
        grad_q = [nn(rows_of(grad_scores, n), keys[n]).astype(BF16) for n in range(len(items))]
        grad_k = [tn(rows_of(grad_scores, n), query[n]).astype(BF16) for n in range(len(items))]
        for n, (h, i) in enumerate(items):
            out = jnp.where(keeps[i], outs[n], 0.0).astype(BF16)
            if h == 0:
                att[zl * NY + sources[i]] = out
                gq[zl * NY + sources[i]] = grad_q[n]
            else:
                out_s[first + i, 0] = out
                out_s[first + i, 1] = grad_q[n]
        both = [jnp.concatenate([grad_k[n], grad_v[n]], axis=1) for n in range(len(items))]
        count = len(sources)
        grads = [both[n * count : (n + 1) * count] for n in range(len(heads))]
        return [g[0] if count == 1 else jnp.concatenate(g, axis=0) for g in grads]

    def pair_tokens(dist):
        lo = 2 * (dist - 1)
        return ring[lo : lo + 2].reshape(256, DI)

    def pair(dist, heads):
        tokens = pair_tokens(dist)
        grads = attend(heads, [y_at(-dist), y_at(dist)], tokens, 2 * dist - 1)
        if len(heads) == 1:
            acc[heads[0]] += tn(tokens, grads[0])
        else:
            term = tn(tokens, jnp.concatenate(grads, axis=1))
            acc[0] += term[:, :256]
            acc[1] += term[:, 256:]

    acc[0] = tn(tok[...], attend((0,), [y], tok[...], 0)[0])

    arrive(1, 0)
    for copy in c1:
        copy.wait_recv()
    c2 = send(remote(prow.at[zl], prow.at[zl], c2_ss, c2_rs, z_peer))
    arrive(1, 1)
    swap_w.wait_recv()
    share_w = send(remote(w.at[1, :, cols], w.at[1, :, cols], w_ss.at[1], w_rs.at[1], c_peer))
    pair(1, (0,))

    arrive(2, 0)
    c2.wait_recv()
    pwide[...] = prow[...].reshape(16, 16, 128).astype(F32)
    part = jnp.zeros((16, HD), F32)
    for i in range(DI // 128):
        part += nn(pwide[:, i, :].astype(BF16), wp[i * 128 : (i + 1) * 128, :])
    gbuf[x, zh, c] = jnp.concatenate([part.astype(BF16), txt[...]], axis=0)
    c3a = send(remote(gbuf.at[x, zh, c], gbuf.at[x, zh, c], c3_ss.at[0], c3_rs.at[0], c_peer))
    swap_q.wait_recv()
    swap_do.wait_recv()
    share_w.wait_recv()
    acc[1] = tn(tok[...], attend((1,), [y], tok[...], 0)[0])
    pair(1, (1,))

    arrive(2, 1)
    c3a.wait_recv()
    c3b = [
        send(remote(gbuf.at[x, zh], gbuf.at[x, zh], c3_ss.at[k], c3_rs.at[k], x_peer(k))) for k in range(1, NX)
    ]
    pair(2, (0, 1))

    arrive(3, 0)
    for copy in c3b:
        copy.wait_recv()
    c3c = [
        send(remote(gbuf.at[:, zh], gbuf.at[:, zh], c3_ss.at[3 + k], c3_rs.at[3 + k], h_peer(k)))
        for k in range(1, NZH)
    ]

    arrive(3, 1)
    pair(3, (0, 1))
    back = [send(remote(out_s.at[0:7], out_r.at[0:7], z_ss.at[2], z_rs.at[2], z_peer))]
    for copy in c3c:
        copy.wait_recv()
    every = gbuf[...].reshape(512 // 16, 32, HD)
    all_img = every[:, :16].reshape(512, HD)
    all_txt = every[:, 16:].reshape(512, HD)
    own = gbuf[x, zh, c]
    dots_img = nt(own[:16], all_txt)
    dots_txt = nt(own[16:], all_img)
    ones = jnp.ones((8, HD), F32)

    def squares(rows_):
        wide = rows_.astype(F32)
        return lax.dot_general(
            ones, wide * wide, (((1,), (1,)), ((), ())),
            preferred_element_type=F32, precision=lax.Precision.HIGHEST,
        )

    sq_img, sq_txt = squares(all_img), squares(all_txt)
    for k in range(NY):
        pk[k, 0:2] = dots_img[2 * k : 2 * k + 2]
        pk[k, 2:4] = dots_txt[2 * k : 2 * k + 2]
        pk[k, 4:6] = sq_img[4:6]
        pk[k, 6:8] = sq_txt[6:8]
    c4 = send(remote(pk, pz, c4_ss, c4_rs, z_peer))

    arrive(4, 0)
    arrive(4, 1)
    tokens = ring[6]
    grads = attend((0, 1), [y_at(4)], tokens, 7)

    XR, HR, CR = DI // NX, DI // (NX * NZH), DI // (NX * NZH * NC)
    keys_part = jnp.concatenate([g[:, :HD] for g in grads], axis=1).astype(F32)
    values_part = jnp.concatenate([g[:, HD:] for g in grads], axis=1).astype(F32)
    theirs = jnp.where(c == 0, values_part, keys_part).astype(BF16)
    ours = jnp.where(c == 0, keys_part, values_part).astype(BF16)
    t1 = []
    for i, (lo, hi) in enumerate(((0, DI),)):
        term = tn(tokens[:, lo:hi], theirs)
        s1[lo:hi, :HD] = (acc[0, lo:hi, cols_there] + term[:, :HD]).astype(BF16)
        s1[lo:hi, HD:] = (acc[1, lo:hi, cols_there] + term[:, HD:]).astype(BF16)
        t1.append(send(remote(s1.at[lo:hi], r1.at[lo:hi], t1_ss.at[i], t1_rs.at[i], c_peer)))
    back.append(send(remote(out_s.at[7], out_r.at[7], z_ss.at[3], z_rs.at[3], z_peer)))
    term = tn(tokens, ours)
    mine[:, :HD] = acc[0, :, cols] + term[:, :HD]
    mine[:, HD:] = acc[1, :, cols] + term[:, HD:]
    c4.wait_recv()
    for k in range(NY):
        pk2[k] = pk[k] + pz[k]
    c5 = [
        send(remote(pk2.at[y_at(k)], rk.at[k], c5_ss.at[k], c5_rs.at[k], y_peer(k))) for k in range(1, NY)
    ]

    def block(k):
        return pl.ds(pl.multiple_of(x_at(k) * XR, 32), XR)

    def over_z(k):
        return remote(s2.at[k], r2.at[k], t2_ss.at[k], t2_rs.at[k], z_peer)

    def over_x(k):
        return remote(s3.at[k], r3.at[k], t3_ss.at[k], t3_rs.at[k], x_peer(k))

    def over_x2(k):
        return remote(s3w.at[k], r3w.at[k], t3_ss.at[k], t3_rs.at[k], x_peer(k))

    order = (2, 1, 3)
    for copy in t1:
        copy.wait_recv()

    @pl.when(c == 0)
    def _():
        for k in order + (0,):
            both = mine[block(k), :] + r1[block(k), :].astype(F32)
            own2[k] = both[:, :HD]
            s2[k] = both[:, HD:].astype(BF16)
            over_z(k).start()

    @pl.when(c == 1)
    def _():
        for k in order:
            s3w[k] = (mine[block(k), :] + r1[block(k), :].astype(F32)).astype(BF16)
            over_x2(k).start()
        own_w[...] = mine[block(0), :] + r1[block(0), :].astype(F32)

    total = pk2[y]
    for k in range(1, NY):
        c5[k - 1].wait_recv()
        total += rk[k]
    spot = lax.broadcasted_iota(jnp.int32, (2, 512), 1)
    index = d * 16 + 2 * y + lax.broadcasted_iota(jnp.int32, (2, 512), 0)
    hit = spot == index
    sq_i, sq_t = total[4:5], total[6:7]

    def side(dots, sq_rows, sq_cols):
        sq_row = jnp.sum(jnp.where(hit, sq_rows, 0.0), axis=1, keepdims=True)
        logits = temp[0] * dots * lax.rsqrt(sq_row + 1e-6) * lax.rsqrt(sq_cols + 1e-6)
        top = jnp.max(logits, axis=1, keepdims=True)
        lse = top + jnp.log(jnp.sum(jnp.exp(logits - top), axis=1, keepdims=True))
        return lse - jnp.sum(jnp.where(hit, logits, 0.0), axis=1, keepdims=True)

    img_side = side(total[0:2], sq_i, sq_t)
    txt_side = side(total[2:4], sq_t, sq_i)
    lane = lax.broadcasted_iota(jnp.int32, (8, 128), 1)
    line = lax.broadcasted_iota(jnp.int32, (8, 128), 0)
    tile = jnp.zeros((8, 128), F32)
    for r in range(2):
        here_lane = lane == 2 * y + r
        tile = jnp.where(here_lane & (line == 0), img_side[r : r + 1], tile)
        tile = jnp.where(here_lane & (line == 1), txt_side[r : r + 1], tile)
    cs[...] = tile
    c6 = [send(remote(cs, cr.at[k], c6_ss.at[k], c6_rs.at[k], y_peer(k))) for k in range(1, NY)]

    @pl.when(c == 0)
    def _():
        for k in order:
            over_z(k).wait_recv()
            s3[k] = (own2[k] + r2[k].astype(F32)).astype(BF16)
            over_x(k).start()
        over_z(0).wait_recv()
        block_sum = own2[0] + r2[0].astype(F32)
        for k in order:
            over_x(k).wait_recv()
            block_sum += r3[k].astype(F32)
        t3[...] = block_sum

    @pl.when(c == 1)
    def _():
        for k in order:
            over_x2(k).wait_recv()
        wide = own_w[...]
        for k in order:
            wide += r3w[k].astype(F32)
        s2[0] = wide[:, HD:].astype(BF16)
        over_z(0).start()
        over_z(0).wait_recv()
        t3[...] = wide[:, :HD] + r2[0].astype(F32)

    t4 = []
    for k in range(1, NZH):
        s4[k, 0:HR] = t3[pl.ds(pl.multiple_of(h_at(k) * HR, 8), HR), :].astype(BF16)
        t4.append(send(remote(s4.at[k], r4.at[k], t4_ss.at[k], t4_rs.at[k], h_peer(k))))
    piece = t3[pl.ds(pl.multiple_of(zh * HR, 8), HR), :]
    for copy in back:
        copy.wait_recv()
    for i, dist in enumerate((0, -1, 1, -2, 2, -3, 3, 4)):
        att[(1 - zl) * NY + y_at(dist)] = out_r[i, 0]
        gq[(1 - zl) * NY + y_at(dist)] = out_r[i, 1]
    answer = cs[...]
    for k in range(1, NY):
        c6[k - 1].wait_recv()
        answer += cr[k]
    con[...] = answer[0:2, 0:16]
    for k in range(1, NZH):
        t4[k - 1].wait_recv()
        piece += r4[k, 0:HR].astype(F32)
    low, high = piece[:CR], piece[CR:]
    s5[0:CR] = jnp.where(c == 0, high, low)
    t5 = send(remote(s5, r5, t5_ss, t5_rs, c_peer))
    kept = jnp.where(c == 0, low, high)

    for copy in sent:
        if copy is not t5:
            copy.wait_send()

    @pl.when(c == 0)
    def _():
        for k in order + (0,):
            over_z(k).wait_send()
        for k in order:
            over_x(k).wait_send()

    @pl.when(c == 1)
    def _():
        for k in order:
            over_x2(k).wait_send()
        over_z(0).wait_send()

    t5.wait_recv()
    got = r5[0:CR]
    dwk[...] = jnp.where(c == 0, kept, got)
    dwv[...] = jnp.where(c == 0, got, kept)
    t5.wait_send()


def body(img_tokens, w_key, w_value, queries, lengths, d_out, img_pooled, w_proj, txt_embed, inv_temp):
    vmem = pl.BlockSpec(memory_space=pltpu.VMEM)
    smem = pl.BlockSpec(memory_space=pltpu.SMEM)
    hbm = pl.BlockSpec(memory_space=pltpu.HBM)
    dma = pltpu.SemaphoreType.DMA
    V = pltpu.VMEM
    ag, dw, con = pl.pallas_call(
        kernel,
        out_shape=(
            jax.ShapeDtypeStruct((2, 16, 32, HD), BF16),
            jax.ShapeDtypeStruct((2, 44, HD), F32),
            jax.ShapeDtypeStruct((2, 16), F32),
        ),
        in_specs=[hbm] * 9 + [smem],
        out_specs=(vmem,) * 3,
        scratch_shapes=[
            V((128, DI), BF16),
            V((16, 32, HD), BF16),
            pltpu.SMEM((16,), jnp.int32),
            V((16, 32, HD), BF16),
            V((1, DI), BF16),
            V((DI, HD), BF16),
            V((16, HD), BF16),
            dma((9,)),
            V((7, 128, DI), BF16),
            V((2, DI, 256), BF16),
            V((8, 32, HD), BF16),
            V((8, 32, HD), BF16),
            V((8, 2, 32, HD), BF16),
            V((8, 2, 32, HD), BF16),
            V((2, DI, 256), F32),
            V((DI, 256), F32),
            V((DI, 256), BF16),
            V((DI, 256), BF16),
            V((4, 352, HD), F32),
            V((4, 352, HD), BF16),
            V((4, 352, HD), BF16),
            V((4, 352, HD), BF16),
            V((4, 352, HD), BF16),
            V((352, 256), F32),
            V((4, 352, 256), BF16),
            V((4, 352, 256), BF16),
            V((352, HD), F32),
            V((4, 96, HD), BF16),
            V((4, 96, HD), BF16),
            V((48, HD), F32),
            V((48, HD), F32),
            V((2, 8, 16, 128), BF16),
            V((16, 16, 128), F32),
            V((4, 4, 2, 32, HD), BF16),
            V((8, 8, 512), F32),
            V((8, 8, 512), F32),
            V((8, 8, 512), F32),
            V((8, 8, 512), F32),
            V((8, 128), F32),
            V((8, 8, 128), F32),
            dma((2, 4, 2)), dma((2, 4, 2)),
            dma((4,)), dma((4,)),
            dma((2,)), dma((2,)),
            dma((8,)), dma((8,)),
            dma, dma,
            dma((7,)), dma((7,)),
            dma, dma,
            dma((8,)), dma((8,)),
            dma((8,)), dma((8,)),
            dma((1,)), dma((1,)),
            dma((4,)), dma((4,)),
            dma((4,)), dma((4,)),
            dma((4,)), dma((4,)),
            dma, dma,
        ],
        compiler_params=pltpu.CompilerParams(
            collective_id=0, has_side_effects=True, vmem_limit_bytes=60 * 1024 * 1024
        ),
        cost_estimate=pl.CostEstimate(flops=6_200_000_000, bytes_accessed=4_000_000, transcendentals=100_000),
    )(
        img_tokens.reshape(128, DI), w_key, w_value, queries, lengths, d_out, img_pooled, w_proj, txt_embed, inv_temp
    )
    return ag[0], ag[1], dw[0], dw[1], con


def solution(mesh):
    placed = (
        P(("dp", "mp"), None, None),
        P(None, "mp"),
        P(None, "mp"),
        P("dp", None, "mp"),
        P("dp"),
        P("dp", None, "mp"),
        P(("dp", "mp"), None),
        P(None, "mp"),
        P("dp", "mp"),
        P(),
    )
    return jax.shard_map(
        body,
        mesh=mesh,
        in_specs=placed,
        out_specs=(
            P("dp", None, "mp"),
            P("dp", None, "mp"),
            P("dp", "mp"),
            P("dp", "mp"),
            P(None, "dp"),
        ),
        check_vma=False,
    )
```
